32 devices in a mesh: farm: 2 (over x), body: 16 (over z, y, core).
Axes of the slice: x: 2, y: 2, z: 4, core: 2. Of those that a mesh axis runs over, the one named last changes fastest.
Arguments:
- incident: float32 [32, 2, 16, 768], P(('farm', 'body')), parts along dimension 0, may hold values from -6 to 6
- self_inverse: float32 [32, 2, 768, 768], P(('farm', 'body')), parts along dimension 0
- cross_blocks: float32 [32, 4, 2, 768, 768], P(('farm', 'body')), parts along dimension 0, may hold values from -0.046875 to 0.046875
- neighbours: int32 [32, 4], P(('farm', 'body')), parts along dimension 0, may hold values from -1 to 15, as said below
- panel_weight: float32 [32, 768], P(('farm', 'body')), parts along dimension 0, may hold values from -0.0546875 to 0.0546875
Outputs:
- sources: float32 [32, 2, 16, 768], P(('farm', 'body')), parts along dimension 0
- farm_force: float32 [2, 2, 16], P('farm'), parts along dimension 0
The draws below stay inside these ranges and needn't reach their ends.
There are 2 independent parts, one for each index of `farm`. The reference program is written for one: setup_inputs(seed, part) draws one part's arguments, and reference() takes and returns one part's arrays. A program takes and returns all parts, laid end to end along the dimension named above; each array names one. Nothing has to cross between parts.
Inputs may be any that keep to these rules, and one draw needn't show every extreme that they name: `neighbours`: each row names distinct bodies other than its own, each within 8 positions of it around the closed loop of 16 bodies; some body names the body exactly 8 positions away.
All inputs are finite; a program needn't handle non-finite values.
Results may differ from the reference program's by a relative error of at most 0.0003.
Values sent between devices are 32-bit elements; how exact they have to be, the bound alone decides.
A program may use at most 128 MiB of HBM per device.

```python
import math
import jax
import jax.numpy as jnp
from jax import lax

PANELS = 768
HEADINGS = 16
SLOTS = 4
ITERS = 6
BODIES = 16
REACH = 8


def draw_self_inverse(key, part):
    key_off, key_diag = jax.random.split(jax.random.fold_in(key, 11))
    shape = (BODIES, 2, PANELS, PANELS)
    off = jax.random.normal(key_off, shape, jnp.float32) * (0.3 / math.sqrt(PANELS))
    diag = jax.random.uniform(key_diag, (BODIES, PANELS), jnp.float32, 0.5, 1.5)
    eye = jnp.arange(PANELS)[:, None] == jnp.arange(PANELS)[None, :]
    real_part = off[:, 0] + jnp.where(eye[None], diag[:, :, None], 0.0)
    return jnp.stack([real_part, off[:, 1]], axis=1).astype(jnp.float32)


def draw_neighbours(key, part):
    key_score, key_row, key_keep = jax.random.split(jax.random.fold_in(key, 23), 3)
    steps_up = jnp.arange(1, REACH + 1, dtype=jnp.int32)
    steps_down = -jnp.arange(1, REACH, dtype=jnp.int32)
    candidates = jnp.concatenate([steps_up, steps_down])
    width = 2 * REACH - 1
    scores = jax.random.randint(key_score, (BODIES, width), 0, 1 << 20) * width + jnp.arange(width, dtype=jnp.int32)[None]
    order = jnp.argsort(scores, axis=1, stable=True)[:, :SLOTS]
    offsets = candidates[order]
    special = jnp.array([REACH, 1, -1, 2], dtype=jnp.int32)[:SLOTS]
    chosen = jax.random.randint(key_row, (), 0, BODIES)
    is_chosen = (jnp.arange(BODIES) == chosen)[:, None]
    offsets = jnp.where(is_chosen, special[None], offsets)
    keep = (jax.random.randint(key_keep, (BODIES, SLOTS), 0, 4) > 0) | is_chosen
    source_index = (jnp.arange(BODIES, dtype=jnp.int32)[:, None] + offsets) % BODIES
    return jnp.where(keep, source_index, -1).astype(jnp.int32)


def block_levels(own_key, shape, shards, low, high):
    loudness = 1.0
    for axis_at, parts in shards:
        steps = jax.random.uniform(jax.random.fold_in(jax.random.fold_in(own_key, 6), axis_at), (parts,), jnp.float32, low / len(shards), high / len(shards))
        loudness = loudness * jnp.repeat(jnp.exp(steps), shape[axis_at] // parts).reshape((-1,) + (1,) * (len(shape) - 1 - axis_at))
    return loudness


def centred(rng, shape, deviation, bound, cuts=(), held_as=jnp.bfloat16):
    level = block_levels(rng, shape, cuts, -0.22, 0.18) if cuts else 1.0
    values = jax.random.normal(rng, shape, jnp.float32) * deviation * level
    return jnp.minimum(jnp.maximum(values, -bound), bound).astype(held_as)


def setup_inputs(seed: int = 0, part: int = 0) -> dict:
    keys = jax.random.split(jax.random.key(seed), 6)
    own_keys = jax.random.split(jax.random.fold_in(keys[5], part), 6)
    incident = centred(own_keys[0], (BODIES, 2, HEADINGS, PANELS), 1.0, 6.0, ((0, 16),), jnp.float32)
    self_inverse = draw_self_inverse(jax.random.fold_in(jax.random.fold_in(keys[5], part), 71), part)
    cross_blocks = centred(own_keys[2], (BODIES, SLOTS, 2, PANELS, PANELS), (25 * PANELS) ** -0.5, 0.046875, ((0, 16),), jnp.float32)
    neighbours = draw_neighbours(jax.random.fold_in(jax.random.fold_in(keys[5], part), 71), part)
    panel_weight = centred(own_keys[4], (BODIES, PANELS), (BODIES * PANELS) ** -0.5, 0.0546875, ((0, 16),), jnp.float32)
    return dict(incident=incident, self_inverse=self_inverse, cross_blocks=cross_blocks, neighbours=neighbours, panel_weight=panel_weight)


def complex_apply(matrix, field):
    heads = field.shape[1]
    stacked = field.reshape(2 * heads, field.shape[2])
    dims = (((1,), (1,)), ((), ()))
    real_part = lax.dot_general(stacked, matrix[0], dims, precision=lax.Precision.HIGHEST)
    imag_part = lax.dot_general(stacked, matrix[1], dims, precision=lax.Precision.HIGHEST)
    return jnp.stack([real_part[:heads] - imag_part[heads:], real_part[heads:] + imag_part[:heads]])


def reference(incident, self_inverse, cross_blocks, neighbours, panel_weight):
    live = neighbours >= 0
    safe = jnp.where(live, neighbours, 0).astype(jnp.int32)
    sources = lax.map(lambda pair: complex_apply(pair[0], pair[1]), (self_inverse, incident))
    for sweep in range(ITERS):
        previous = sources

        def update(items):
            inverse_one, blocks, field, index_row, flag_row = items
            total = field
            for slot in range(SLOTS):
                other = lax.dynamic_index_in_dim(previous, index_row[slot], 0, keepdims=False)
                total = total - jnp.where(flag_row[slot], complex_apply(blocks[slot], other), 0.0)
            return complex_apply(inverse_one, total)

        sources = lax.map(update, (self_inverse, cross_blocks, incident, safe, live))
    force = jnp.einsum("bp,bchp->ch", panel_weight, sources, precision=lax.Precision.HIGHEST)
    return sources, force[None]
```

```python
import functools

import jax
import jax.numpy as jnp
from jax import lax
from jax.experimental import pallas as pl
from jax.experimental.pallas import tpu as pltpu
from jax.sharding import PartitionSpec as P

ITERS = 6
TILE = 256
VIA = (2,)
F32 = jnp.float32
BF16 = jnp.bfloat16


def flip(index, bits):
    bit = 1
    while bit <= bits:
        if bits & bit:
            index = index + bit - 2 * bit * ((index // bit) % 2)
        bit *= 2
    return index


def differ(first, second, bodies):
    total, bit = 0, 1
    while bit < bodies:
        total = total + bit * (((first // bit) + (second // bit)) % 2)
        bit *= 2
    return total


def halves(value):
    high = value.astype(BF16)
    return high, (value - high.astype(F32)).astype(BF16)


def put_field(lhs, column, value, heads):
    rows, width = value.shape
    high, low = halves(value)
    high_t = jnp.concatenate([-high[heads:], high[:heads]], axis=0)
    low_t = jnp.concatenate([-low[heads:], low[:heads]], axis=0)
    lhs[0:rows, column : column + width] = high
    lhs[rows : 2 * rows, column : column + width] = low
    lhs[0:rows, column + width : column + 2 * width] = high_t
    lhs[rows : 2 * rows, column + width : column + 2 * width] = low_t


def multiply(lhs, base, depth, high, low, at, rows):
    deep = slice(base, base + depth)
    both = jnp.dot(lhs[:, 0:depth], high[deep, at], preferred_element_type=F32)
    small = jnp.dot(lhs[0:rows, 0:depth], low[deep, at], preferred_element_type=F32)
    return both[:rows] + both[rows:] + small


def routes(bodies):
    far = [bit for bit in (2**k for k in range(20)) if 4 <= bit < bodies][::-1]
    masks = sorted(
        {sum(bit for j, bit in enumerate(far) if pick >> j & 1) for pick in range(1, 2 ** len(far))},
        key=lambda mask: (bin(mask).count("1"), -mask),
    )
    return far, masks


def kernel(
    bodies, slots, heads, panels,
    neighbours, incident, inverse, blocks, weight,
    out, force,
    stage, inv_high, inv_low, cross_high, cross_low, lhs, lhs_own, product, shares,
    load_sem, send_sem, recv_sem, share_send, share_recv, *gathered,
):
    rows = 2 * heads
    me = lax.axis_index("body")
    count = panels // TILE
    cuts = [slice(start, start + TILE) for start in range(0, panels, TILE)]
    far, masks = routes(bodies)
    last_side = masks[-1] + 2

    def load(index):
        source = inverse.at[0, index] if index < 2 else blocks.at[0, (index - 2) // 2, (index - 2) % 2]
        return pltpu.make_async_copy(source, stage.at[index], load_sem.at[index])

    for index in range(2):
        load(index).start()

    barrier = pltpu.get_barrier_semaphore()
    for bits in range(1, bodies):
        pl.semaphore_signal(barrier, inc=1, device_id={"body": flip(me, bits)})

    for index in range(2, 2 + 2 * slots):
        load(index).start()

    def split(index, high, low, part, parts):
        load(index).wait()

        @pl.loop(0, panels // 128)
        def _(step):
            at = pl.ds(pl.multiple_of(step * 128, 128), 128)
            upper, lower = halves(stage[index, at, :].T)
            for piece, cut in enumerate(cuts):
                to = parts * cut.start + part * TILE
                high[to : to + TILE, at] = upper[cut]
                low[to : to + TILE, at] = lower[cut]

    def copy(parity, mask, bit, piece):
        return pltpu.make_async_remote_copy(
            src_ref=gathered[parity * count + piece].at[mask],
            dst_ref=gathered[parity * count + piece].at[mask ^ bit],
            send_sem=send_sem.at[bit.bit_length() - 1, mask, piece],
            recv_sem=recv_sem.at[parity, mask ^ bit, piece],
            device_id={"body": flip(me, bit)},
        )

    def wait_in(parity, mask, piece):
        copy(parity, mask ^ 1, 1, piece).wait_recv()

    def onward(mask, piece):
        if mask & 1:
            return []
        if mask & 2:
            return [far[-1], 1] if mask == last_side ^ far[-1] and piece in VIA else [1]
        if mask == last_side ^ 2 and piece in VIA:
            return [1]
        low = mask & -mask if mask else 2**20
        return [bit for bit in far if bit < low] + [2, 1]

    def start(parity, mask, piece):
        for bit in onward(mask, piece):
            copy(parity, mask, bit, piece).start()

    def relay(parity, mask, piece):
        wait_in(parity, mask, piece)
        start(parity, mask, piece)

    def drain(parity, mask):
        for piece in range(count):
            for bit in onward(mask, piece):
                copy(parity, mask, bit, piece).wait_send()

    def solve(parity, value):
        for piece, cut in enumerate(cuts):
            put_field(lhs_own, 2 * cut.start, value[:, cut], heads)
        for piece, cut in enumerate(cuts):
            part = multiply(lhs_own, 0, 2 * panels, inv_high, inv_low, cut, rows)
            if parity is None:
                product[:, cut] = part
            else:
                gathered[parity * count + piece][0] = part
                start(parity, 0, piece)

    names = [neighbours[0, slot] for slot in range(slots)]
    places = [differ(jnp.maximum(name, 0), me, bodies) for name in names]

    def consume(parity, piece):
        for mask in range(1, bodies, 2):
            wait_in(parity, mask, piece)
        for slot in range(slots):
            value = gathered[parity * count + piece][places[slot]]
            put_field(lhs, 2 * slot * TILE, jnp.where(names[slot] >= 0, value, 0.0), heads)
        depth = 2 * slots * TILE
        for cut in cuts:
            part = multiply(lhs, 2 * slots * cuts[piece].start, depth, cross_high, cross_low, cut, rows)
            before = incident[0, :, :, cut].reshape(rows, TILE) if piece == 0 else product[:, cut]
            product[:, cut] = before - part

    for part in range(2):
        split(part, inv_high, inv_low, part, 2)
    pl.semaphore_wait(barrier, bodies - 1)
    solve(0, incident[0].reshape(rows, panels))

    stages = [masks[: len(far)], masks[len(far) :]]
    sides = [mask + 2 for mask in masks]
    sides = [mask for mask in sides if mask == last_side ^ far[-1]] + [2] + [mask for mask in sides if mask != last_side ^ far[-1]]

    def sweep(parity, pair):
        def first(parts):
            if parity == 0:
                @pl.when(pair == 0)
                def _():
                    for part in parts:
                        split(2 + part, cross_high, cross_low, part, 2 * slots)

        total = 2 * slots
        marks = [0, (3 * total) // 8, (6 * total) // 8, total]
        first(range(marks[0], marks[1]))
        for mask in stages[0]:
            for piece in range(count):
                relay(parity, mask, piece)
        first(range(marks[1], marks[2]))
        for mask in stages[1]:
            for piece in range(count):
                relay(parity, mask, piece)
        first(range(marks[2], marks[3]))
        for mask in sides[:-1]:
            for piece in range(count):
                relay(parity, mask, piece)
        drain(parity, 0)
        for mask in stages[0]:
            drain(parity, mask)
        last = sides[-1]
        for piece in range(count):
            relay(parity, last, piece)
        for piece in range(count):
            consume(parity, piece)
        for mask in stages[1] + sides:
            drain(parity, mask)

    @pl.loop(0, ITERS // 2)
    def _(pair):
        sweep(0, pair)
        solve(1, product[...])
        sweep(1, pair)

        @pl.when(pair < ITERS // 2 - 1)
        def _():
            solve(0, product[...])

    solve(None, product[...])
    final = product[...]
    out[0] = final.reshape(2, heads, panels)
    scale = jnp.broadcast_to(weight[...], (8, panels))
    sums = [
        lax.dot_general(
            scale, final[c * heads : (c + 1) * heads], (((1,), (1,)), ((), ())),
            precision=lax.Precision.HIGHEST, preferred_element_type=F32,
        )
        for c in range(2)
    ]
    row = lax.broadcasted_iota(jnp.int32, (8, heads), 0)
    shares[0] = jnp.zeros((8, 128), F32)
    shares[0, :, 0:heads] = jnp.where(row == 0, sums[0], sums[1])

    def share(bits):
        return pltpu.make_async_remote_copy(
            src_ref=shares.at[0],
            dst_ref=shares.at[bits],
            send_sem=share_send.at[bits],
            recv_sem=share_recv.at[bits],
            device_id={"body": flip(me, bits)},
        )

    for bits in range(1, bodies):
        share(bits).start()
    for bits in range(1, bodies):
        share(bits).wait_recv()
    total = jnp.zeros((8, 128), F32)
    for body in range(bodies):
        total = total + shares[differ(me, body, bodies)]
    force[0] = total[0:2, 0:heads]
    for bits in range(1, bodies):
        share(bits).wait_send()


def solution(mesh):
    bodies = mesh.shape["body"]

    def step(incident, self_inverse, cross_blocks, neighbours, panel_weight):
        heads, panels = incident.shape[2:]
        slots = neighbours.shape[1]
        rows = 2 * heads
        count = panels // TILE
        vmem = pl.BlockSpec(memory_space=pltpu.VMEM)
        anywhere = pl.BlockSpec(memory_space=pl.ANY)
        return pl.pallas_call(
            functools.partial(kernel, bodies, slots, heads, panels),
            out_shape=(
                jax.ShapeDtypeStruct(incident.shape, F32),
                jax.ShapeDtypeStruct((1, 2, heads), F32),
            ),
            in_specs=[pl.BlockSpec(memory_space=pltpu.SMEM), vmem, anywhere, anywhere, vmem],
            out_specs=(vmem, vmem),
            scratch_shapes=[
                pltpu.VMEM((2 + 2 * slots, panels, panels), F32),
                pltpu.VMEM((2 * panels, panels), BF16),
                pltpu.VMEM((2 * panels, panels), BF16),
                pltpu.VMEM((2 * slots * panels, panels), BF16),
                pltpu.VMEM((2 * slots * panels, panels), BF16),
                pltpu.VMEM((2 * rows, 2 * slots * TILE), BF16),
                pltpu.VMEM((2 * rows, 2 * panels), BF16),
                pltpu.VMEM((rows, panels), F32),
                pltpu.VMEM((bodies, 8, 128), F32),
                pltpu.SemaphoreType.DMA((2 + 2 * slots,)),
                pltpu.SemaphoreType.DMA((bodies.bit_length(), bodies, count)),
                pltpu.SemaphoreType.DMA((2, bodies, count)),
                pltpu.SemaphoreType.DMA((bodies,)),
                pltpu.SemaphoreType.DMA((bodies,)),
                *[pltpu.VMEM((bodies, rows, TILE), F32)] * (2 * count),
            ],
            compiler_params=pltpu.CompilerParams(
                collective_id=0, has_side_effects=True, vmem_limit_bytes=60 * 1024 * 1024
            ),
        )(neighbours, incident, self_inverse, cross_blocks, panel_weight)

    return jax.shard_map(
        step,
        mesh=mesh,
        in_specs=(
            P(("farm", "body"), None, None, None),
            P(("farm", "body"), None, None, None),
            P(("farm", "body"), None, None, None, None),
            P(("farm", "body"), None),
            P(("farm", "body"), None),
        ),
        out_specs=(P(("farm", "body"), None, None, None), P("farm", None, None)),
        check_vma=False,
    )
```

```python
import functools

import jax
import jax.numpy as jnp
from jax import lax
from jax.experimental import pallas as pl
from jax.experimental.pallas import tpu as pltpu
from jax.sharding import PartitionSpec as P

ITERS = 6
TILE = 256
VIA = (2,)
F32 = jnp.float32
BF16 = jnp.bfloat16


def flip(index, bits):
    bit = 1
    while bit <= bits:
        if bits & bit:
            index = index + bit - 2 * bit * ((index // bit) % 2)
        bit *= 2
    return index


def differ(first, second, bodies):
    total, bit = 0, 1
    while bit < bodies:
        total = total + bit * (((first // bit) + (second // bit)) % 2)
        bit *= 2
    return total


def halves(value):
    high = value.astype(BF16)
    return high, (value - high.astype(F32)).astype(BF16)


def put_field(lhs, column, value, heads):
    rows, width = value.shape
    high, low = halves(value)
    high_t = jnp.concatenate([-high[heads:], high[:heads]], axis=0)
    low_t = jnp.concatenate([-low[heads:], low[:heads]], axis=0)
    lhs[0:rows, column : column + width] = high
    lhs[rows : 2 * rows, column : column + width] = low
    lhs[0:rows, column + width : column + 2 * width] = high_t
    lhs[rows : 2 * rows, column + width : column + 2 * width] = low_t


def multiply(lhs, base, depth, high, low, at, rows):
    deep = slice(base, base + depth)
    both = jnp.dot(lhs[:, 0:depth], high[deep, at], preferred_element_type=F32)
    small = jnp.dot(lhs[0:rows, 0:depth], low[deep, at], preferred_element_type=F32)
    return both[:rows] + both[rows:] + small


def routes(bodies):
    far = [bit for bit in (2**k for k in range(20)) if 4 <= bit < bodies][::-1]
    masks = sorted(
        {sum(bit for j, bit in enumerate(far) if pick >> j & 1) for pick in range(1, 2 ** len(far))},
        key=lambda mask: (bin(mask).count("1"), -mask),
    )
    return far, masks


def kernel(
    bodies, slots, heads, panels,
    neighbours, incident, inverse, blocks, weight,
    out, force,
    stage, inv_high, inv_low, cross_high, cross_low, lhs, lhs_own, product, final, shares,
    scale, sums, pull, tally,
    load_sem, send_sem, recv_sem, share_send, share_recv, *gathered,
):
    rows = 2 * heads
    me = lax.axis_index("body")
    count = panels // TILE
    cuts = [slice(start, start + TILE) for start in range(0, panels, TILE)]
    far, masks = routes(bodies)
    last_side = masks[-1] + 2

    def load(index):
        source = inverse.at[0, index] if index < 2 else blocks.at[0, (index - 2) // 2, (index - 2) % 2]
        return pltpu.make_async_copy(source, stage.at[index], load_sem.at[index])

    for index in range(2):
        load(index).start()

    barrier = pltpu.get_barrier_semaphore()
    for bits in range(1, bodies):
        pl.semaphore_signal(barrier, inc=1, device_id={"body": flip(me, bits)})

    for index in range(2, 2 + 2 * slots):
        load(index).start()

    def split(index, high, low, part, parts):
        load(index).wait()

        @pl.loop(0, panels // 128)
        def _(step):
            at = pl.ds(pl.multiple_of(step * 128, 128), 128)
            upper, lower = halves(stage[index, at, :].T)
            for piece, cut in enumerate(cuts):
                to = parts * cut.start + part * TILE
                high[to : to + TILE, at] = upper[cut]
                low[to : to + TILE, at] = lower[cut]

    def copy(parity, mask, bit, piece):
        return pltpu.make_async_remote_copy(
            src_ref=gathered[parity * count + piece].at[mask],
            dst_ref=gathered[parity * count + piece].at[mask ^ bit],
            send_sem=send_sem.at[bit.bit_length() - 1, mask, piece],
            recv_sem=recv_sem.at[parity, mask ^ bit, piece],
            device_id={"body": flip(me, bit)},
        )

    def wait_in(parity, mask, piece):
        copy(parity, mask ^ 1, 1, piece).wait_recv()

    def onward(mask, piece):
        if mask & 1:
            return []
        if mask & 2:
            return [far[-1], 1] if mask == last_side ^ far[-1] and piece in VIA else [1]
        if mask == last_side ^ 2 and piece in VIA:
            return [1]
        low = mask & -mask if mask else 2**20
        return [bit for bit in far if bit < low] + [2, 1]

    def start(parity, mask, piece):
        for bit in onward(mask, piece):
            copy(parity, mask, bit, piece).start()

    def relay(parity, mask, piece):
        wait_in(parity, mask, piece)
        start(parity, mask, piece)

    def drain(parity, mask):
        for piece in range(count):
            for bit in onward(mask, piece):
                copy(parity, mask, bit, piece).wait_send()

    def turn(parity, act):
        for each in range(2):
            pl.when(parity == each)(functools.partial(act, each))

    def solve(sweep, parity):
        value = product[...]
        for piece, cut in enumerate(cuts):
            put_field(lhs_own, 2 * cut.start, value[:, cut], heads)
        for piece, cut in enumerate(cuts):
            part = multiply(lhs_own, 0, 2 * panels, inv_high, inv_low, cut, rows)
            final[:, :, cut] = part.reshape(2, heads, TILE)

            @pl.when(sweep < ITERS)
            def _():
                def send(each):
                    gathered[each * count + piece][0] = part
                    start(each, 0, piece)

                turn(parity, send)

    names = [neighbours[0, slot] for slot in range(slots)]
    places = [differ(jnp.maximum(name, 0), me, bodies) for name in names]

    def set_scale(value):
        scale[0:8], scale[8:16] = halves(value)

    def weigh(index):
        sums[...] = jnp.zeros_like(sums)

        @pl.loop(0, count)
        def _(step):
            at = pl.ds(pl.multiple_of(step * TILE, TILE), TILE)
            upper, lower = halves(stage[index, at, :])
            both = jnp.dot(scale[:, at], upper, preferred_element_type=F32)
            small = jnp.dot(scale[0:8, at], lower, preferred_element_type=F32)
            sums[...] += both[0:8] + both[8:16] + small

        return sums[...]

    top = lax.broadcasted_iota(jnp.int32, (8, panels), 0) == 0

    def pulled(slot, value, cut):
        turned = jnp.concatenate([-value[heads:], value[:heads]], axis=0)
        return pull[slot, 0:1, cut] * value + pull[slot, 1:2, cut] * turned

    def pull_own():
        set_scale(jnp.broadcast_to(weight[...], (8, panels)))
        real = weigh(0)
        pull[0] = jnp.where(top, real, weigh(1))
        set_scale(pull[0])
        tally[...] = pulled(0, incident[0].reshape(rows, panels), slice(0, panels))

    def pull_slot(slot):
        real, imag = weigh(2 + 2 * slot), weigh(3 + 2 * slot)
        pull[1 + slot] = jnp.where(top, real[0:1] - imag[1:2], imag[0:1] + real[1:2])

    def share(bits):
        return pltpu.make_async_remote_copy(
            src_ref=shares.at[0],
            dst_ref=shares.at[bits],
            send_sem=share_send.at[bits],
            recv_sem=share_recv.at[bits],
            device_id={"body": flip(me, bits)},
        )

    def arrive(parity, piece):
        for mask in range(1, bodies, 2):
            wait_in(parity, mask, piece)

    def held(parity, piece, slot):
        value = gathered[parity * count + piece][places[slot]]
        return jnp.where(names[slot] >= 0, value, 0.0)

    LAST = (ITERS - 1) % 2

    def send_share():
        for piece, cut in enumerate(cuts):
            arrive(LAST, piece)
            value = tally[:, cut]
            for slot in range(slots):
                value = value - pulled(1 + slot, held(LAST, piece, slot), cut)
            tally[:, cut] = value
        ones = jnp.ones((8, panels), F32)
        real, imag = [
            lax.dot_general(
                ones, tally[c * heads : (c + 1) * heads], (((1,), (1,)), ((), ())),
                precision=lax.Precision.HIGHEST, preferred_element_type=F32,
            )
            for c in range(2)
        ]
        row = lax.broadcasted_iota(jnp.int32, (8, heads), 0)
        shares[0] = jnp.zeros((8, 128), F32)
        shares[0, :, 0:heads] = jnp.where(row == 0, real, imag)
        for bits in range(1, bodies):
            share(bits).start()

    def consume(sweep, parity, piece):
        def take(each):
            if each == LAST:
                pl.when(sweep < ITERS - 1)(lambda: arrive(each, piece))
            else:
                arrive(each, piece)
            for slot in range(slots):
                put_field(lhs, 2 * slot * TILE, held(each, piece, slot), heads)

        turn(parity, take)
        depth = 2 * slots * TILE
        for cut in cuts:
            part = multiply(lhs, 2 * slots * cuts[piece].start, depth, cross_high, cross_low, cut, rows)
            before = incident[0, :, :, cut].reshape(rows, TILE) if piece == 0 else product[:, cut]
            product[:, cut] = before - part

    for part in range(2):
        split(part, inv_high, inv_low, part, 2)
    pl.semaphore_wait(barrier, bodies - 1)
    product[...] = incident[0].reshape(rows, panels)

    stages = [masks[: len(far)], masks[len(far) :]]
    sides = [mask + 2 for mask in masks]
    sides = [mask for mask in sides if mask == last_side ^ far[-1]] + [2] + [mask for mask in sides if mask != last_side ^ far[-1]]

    def exchange(sweep, parity):
        def first(parts):
            @pl.when(sweep == 0)
            def _():
                for part in parts:
                    split(2 + part, cross_high, cross_low, part, 2 * slots)

        def relays(some):
            def act(each):
                for mask in some:
                    for piece in range(count):
                        relay(each, mask, piece)

            turn(parity, act)

        total = 2 * slots
        first(range(0, (3 * total) // 8))
        for slot in range(slots):
            pl.when(sweep == 1 + slot % (ITERS - 2))(functools.partial(pull_slot, slot))
        relays(stages[0])
        first(range((3 * total) // 8, (6 * total) // 8))
        relays(stages[1])
        first(range((6 * total) // 8, total))
        pl.when(sweep == 0)(pull_own)
        relays(sides[:-1])
        for mask in [0] + stages[0]:
            drain(0, mask)
        relays(sides[-1:])
        pl.when(sweep == ITERS - 1)(send_share)
        for piece in range(count):
            consume(sweep, parity, piece)
        for mask in stages[1] + sides:
            drain(0, mask)

    @pl.loop(0, ITERS + 1)
    def _(sweep):
        parity = lax.rem(sweep, 2)
        solve(sweep, parity)
        pl.when(sweep < ITERS)(lambda: exchange(sweep, parity))

    save = pltpu.make_async_copy(final, out.at[0], load_sem.at[0])
    save.start()
    for bits in range(1, bodies):
        share(bits).wait_recv()
    total = jnp.zeros((8, 128), F32)
    for body in range(bodies):
        total = total + shares[differ(me, body, bodies)]
    force[0] = total[0:2, 0:heads]
    for bits in range(1, bodies):
        share(bits).wait_send()
    save.wait()


def solution(mesh):
    bodies = mesh.shape["body"]

    def step(incident, self_inverse, cross_blocks, neighbours, panel_weight):
        heads, panels = incident.shape[2:]
        slots = neighbours.shape[1]
        rows = 2 * heads
        count = panels // TILE
        vmem = pl.BlockSpec(memory_space=pltpu.VMEM)
        anywhere = pl.BlockSpec(memory_space=pl.ANY)
        return pl.pallas_call(
            functools.partial(kernel, bodies, slots, heads, panels),
            out_shape=(
                jax.ShapeDtypeStruct(incident.shape, F32),
                jax.ShapeDtypeStruct((1, 2, heads), F32),
            ),
            in_specs=[pl.BlockSpec(memory_space=pltpu.SMEM), vmem, anywhere, anywhere, vmem],
            out_specs=(anywhere, vmem),
            scratch_shapes=[
                pltpu.VMEM((2 + 2 * slots, panels, panels), F32),
                pltpu.VMEM((2 * panels, panels), BF16),
                pltpu.VMEM((2 * panels, panels), BF16),
                pltpu.VMEM((2 * slots * panels, panels), BF16),
                pltpu.VMEM((2 * slots * panels, panels), BF16),
                pltpu.VMEM((2 * rows, 2 * slots * TILE), BF16),
                pltpu.VMEM((2 * rows, 2 * panels), BF16),
                pltpu.VMEM((rows, panels), F32),
                pltpu.VMEM((2, heads, panels), F32),
                pltpu.VMEM((bodies, 8, 128), F32),
                pltpu.VMEM((16, panels), BF16),
                pltpu.VMEM((8, panels), F32),
                pltpu.VMEM((1 + slots, 8, panels), F32),
                pltpu.VMEM((rows, panels), F32),
                pltpu.SemaphoreType.DMA((2 + 2 * slots,)),
                pltpu.SemaphoreType.DMA((bodies.bit_length(), bodies, count)),
                pltpu.SemaphoreType.DMA((2, bodies, count)),
                pltpu.SemaphoreType.DMA((bodies,)),
                pltpu.SemaphoreType.DMA((bodies,)),
                *[pltpu.VMEM((bodies, rows, TILE), F32)] * (2 * count),
            ],
            compiler_params=pltpu.CompilerParams(
                collective_id=0, has_side_effects=True, vmem_limit_bytes=60 * 1024 * 1024
            ),
        )(neighbours, incident, self_inverse, cross_blocks, panel_weight)

    return jax.shard_map(
        step,
        mesh=mesh,
        in_specs=(
            P(("farm", "body"), None, None, None),
            P(("farm", "body"), None, None, None),
            P(("farm", "body"), None, None, None, None),
            P(("farm", "body"), None),
            P(("farm", "body"), None),
        ),
        out_specs=(P(("farm", "body"), None, None, None), P("farm", None, None)),
        check_vma=False,
    )
```

```python
import functools

import jax
import jax.numpy as jnp
from jax import lax
from jax.experimental import pallas as pl
from jax.experimental.pallas import tpu as pltpu
from jax.sharding import PartitionSpec as P

ITERS = 6
TILE = 256
VIA = (2,)
F32 = jnp.float32
BF16 = jnp.bfloat16


def flip(index, bits):
    bit = 1
    while bit <= bits:
        if bits & bit:
            index = index + bit - 2 * bit * ((index // bit) % 2)
        bit *= 2
    return index


def differ(first, second, bodies):
    total, bit = 0, 1
    while bit < bodies:
        total = total + bit * (((first // bit) + (second // bit)) % 2)
        bit *= 2
    return total


def halves(value):
    high = value.astype(BF16)
    return high, (value - high.astype(F32)).astype(BF16)


def put_field(lhs, column, value, heads):
    rows, width = value.shape
    high, low = halves(value)
    high_t = jnp.concatenate([-high[heads:], high[:heads]], axis=0)
    low_t = jnp.concatenate([-low[heads:], low[:heads]], axis=0)
    lhs[0:rows, column : column + width] = high
    lhs[rows : 2 * rows, column : column + width] = low
    lhs[0:rows, column + width : column + 2 * width] = high_t
    lhs[rows : 2 * rows, column + width : column + 2 * width] = low_t


def multiply(lhs, base, depth, high, low, at, rows):
    deep = slice(base, base + depth)
    both = jnp.dot(lhs[:, 0:depth], high[deep, at], preferred_element_type=F32)
    small = jnp.dot(lhs[0:rows, 0:depth], low[deep, at], preferred_element_type=F32)
    return both[:rows] + both[rows:] + small


def routes(bodies):
    far = [bit for bit in (2**k for k in range(20)) if 4 <= bit < bodies][::-1]
    masks = sorted(
        {sum(bit for j, bit in enumerate(far) if pick >> j & 1) for pick in range(1, 2 ** len(far))},
        key=lambda mask: (bin(mask).count("1"), -mask),
    )
    return far, masks


def kernel(
    bodies, slots, heads, panels,
    neighbours, incident, inverse, blocks, weight,
    out, force,
    stage, inv_high, inv_low, cross_high, cross_low, lhs, lhs_own, product, final, shares,
    scale, sums, pull, tally,
    load_sem, send_sem, recv_sem, share_send, share_recv, *gathered,
):
    rows = 2 * heads
    me = lax.axis_index("body")
    count = panels // TILE
    cuts = [slice(start, start + TILE) for start in range(0, panels, TILE)]
    far, masks = routes(bodies)
    last_side = masks[-1] + 2

    def load(index):
        source = inverse.at[0, index] if index < 2 else blocks.at[0, (index - 2) // 2, (index - 2) % 2]
        return pltpu.make_async_copy(source, stage.at[index], load_sem.at[index])

    for index in range(2):
        load(index).start()

    barrier = pltpu.get_barrier_semaphore()
    for bits in range(1, bodies):
        pl.semaphore_signal(barrier, inc=1, device_id={"body": flip(me, bits)})

    for index in range(2, 2 + 2 * slots):
        load(index).start()

    def split(index, high, low, part, parts):
        load(index).wait()

        @pl.loop(0, panels // 128)
        def _(step):
            at = pl.ds(pl.multiple_of(step * 128, 128), 128)
            upper, lower = halves(stage[index, at, :].T)
            for piece, cut in enumerate(cuts):
                to = parts * cut.start + part * TILE
                high[to : to + TILE, at] = upper[cut]
                low[to : to + TILE, at] = lower[cut]

    def copy(parity, mask, bit, piece):
        return pltpu.make_async_remote_copy(
            src_ref=gathered[parity * count + piece].at[mask],
            dst_ref=gathered[parity * count + piece].at[mask ^ bit],
            send_sem=send_sem.at[bit.bit_length() - 1, mask, piece],
            recv_sem=recv_sem.at[parity, mask ^ bit, piece],
            device_id={"body": flip(me, bit)},
        )

    def wait_in(parity, mask, piece):
        copy(parity, mask ^ 1, 1, piece).wait_recv()

    def onward(mask, piece):
        if mask & 1:
            return []
        if mask & 2:
            return [far[-1], 1] if mask == last_side ^ far[-1] and piece in VIA else [1]
        if mask == last_side ^ 2 and piece in VIA:
            return [1]
        low = mask & -mask if mask else 2**20
        return [bit for bit in far if bit < low] + [2, 1]

    def start(parity, mask, piece):
        for bit in onward(mask, piece):
            copy(parity, mask, bit, piece).start()

    def relay(parity, mask, piece):
        wait_in(parity, mask, piece)
        start(parity, mask, piece)

    def drain(parity, mask):
        for piece in range(count):
            for bit in onward(mask, piece):
                copy(parity, mask, bit, piece).wait_send()

    def turn(parity, act):
        for each in range(2):
            pl.when(parity == each)(functools.partial(act, each))

    def solve(sweep, parity):
        value = product[...]
        for piece, cut in enumerate(cuts):
            put_field(lhs_own, 2 * cut.start, value[:, cut], heads)
        for piece, cut in enumerate(cuts):
            part = multiply(lhs_own, 0, 2 * panels, inv_high, inv_low, cut, rows)
            final[:, :, cut] = part.reshape(2, heads, TILE)

            @pl.when(sweep < ITERS)
            def _():
                def send(each):
                    gathered[each * count + piece][0] = part
                    start(each, 0, piece)

                turn(parity, send)

    names = [neighbours[0, slot] for slot in range(slots)]
    places = [differ(jnp.maximum(name, 0), me, bodies) for name in names]

    def set_scale(value):
        scale[0:8], scale[8:16] = halves(value)

    def weigh(index):
        sums[...] = jnp.zeros_like(sums)

        @pl.loop(0, count)
        def _(step):
            at = pl.ds(pl.multiple_of(step * TILE, TILE), TILE)
            upper, lower = halves(stage[index, at, :])
            both = jnp.dot(scale[:, at], upper, preferred_element_type=F32)
            small = jnp.dot(scale[0:8, at], lower, preferred_element_type=F32)
            sums[...] += both[0:8] + both[8:16] + small

        return sums[...]

    top = lax.broadcasted_iota(jnp.int32, (8, panels), 0) == 0

    def pulled(slot, value, cut):
        turned = jnp.concatenate([-value[heads:], value[:heads]], axis=0)
        return pull[slot, 0:1, cut] * value + pull[slot, 1:2, cut] * turned

    def pull_own():
        set_scale(jnp.broadcast_to(weight[...], (8, panels)))
        real = weigh(0)
        pull[0] = jnp.where(top, real, weigh(1))
        set_scale(pull[0])
        tally[...] = pulled(0, incident[0].reshape(rows, panels), slice(0, panels))

    def pull_slot(slot):
        real, imag = weigh(2 + 2 * slot), weigh(3 + 2 * slot)
        pull[1 + slot] = jnp.where(top, real[0:1] - imag[1:2], imag[0:1] + real[1:2])

    def share(bits):
        return pltpu.make_async_remote_copy(
            src_ref=shares.at[0],
            dst_ref=shares.at[bits],
            send_sem=share_send.at[bits],
            recv_sem=share_recv.at[bits],
            device_id={"body": flip(me, bits)},
        )

    def arrive(parity, piece):
        for mask in range(1, bodies, 2):
            wait_in(parity, mask, piece)

    def held(parity, piece, slot):
        value = gathered[parity * count + piece][places[slot]]
        return jnp.where(names[slot] >= 0, value, 0.0)

    LAST = (ITERS - 1) % 2

    def send_share():
        for piece, cut in enumerate(cuts):
            arrive(LAST, piece)
            value = tally[:, cut]
            for slot in range(slots):
                value = value - pulled(1 + slot, held(LAST, piece, slot), cut)
            tally[:, cut] = value
        ones = jnp.ones((8, panels), F32)
        real, imag = [
            lax.dot_general(
                ones, tally[c * heads : (c + 1) * heads], (((1,), (1,)), ((), ())),
                precision=lax.Precision.HIGHEST, preferred_element_type=F32,
            )
            for c in range(2)
        ]
        row = lax.broadcasted_iota(jnp.int32, (8, heads), 0)
        shares[0] = jnp.zeros((8, 128), F32)
        shares[0, :, 0:heads] = jnp.where(row == 0, real, imag)
        for bits in range(1, bodies):
            share(bits).start()

    def consume(sweep, parity, piece):
        def take(each):
            if each == LAST:
                pl.when(sweep < ITERS - 1)(lambda: arrive(each, piece))
            else:
                arrive(each, piece)
            for slot in range(slots):
                put_field(lhs, 2 * slot * TILE, held(each, piece, slot), heads)

        turn(parity, take)
        depth = 2 * slots * TILE
        for cut in cuts:
            part = multiply(lhs, 2 * slots * cuts[piece].start, depth, cross_high, cross_low, cut, rows)
            before = incident[0, :, :, cut].reshape(rows, TILE) if piece == 0 else product[:, cut]
            product[:, cut] = before - part

    for part in range(2):
        split(part, inv_high, inv_low, part, 2)
    pl.semaphore_wait(barrier, bodies - 1)
    product[...] = incident[0].reshape(rows, panels)

    stages = [masks[: len(far)], masks[len(far) :]]
    sides = [mask + 2 for mask in masks]
    sides = [mask for mask in sides if mask == last_side ^ far[-1]] + [2] + [mask for mask in sides if mask != last_side ^ far[-1]]

    def exchange(sweep, parity):
        def first(parts):
            @pl.when(sweep == 0)
            def _():
                for part in parts:
                    split(2 + part, cross_high, cross_low, part, 2 * slots)

        def relays(some, which=range(count)):
            def act(each):
                for piece in which:
                    for mask in some:
                        relay(each, mask, piece)

            turn(parity, act)

        total = 2 * slots
        first(range(0, (3 * total) // 8))
        for slot in range(slots):
            pl.when(sweep == 1 + slot % (ITERS - 2))(functools.partial(pull_slot, slot))
        relays(stages[0])
        first(range((3 * total) // 8, (6 * total) // 8))
        relays(stages[1])
        first(range((6 * total) // 8, total))
        pl.when(sweep == 0)(pull_own)
        relays(sides[:-1])
        for mask in [0] + stages[0]:
            drain(0, mask)
        rear = range(count - 1, count)
        relays(sides[-1:], range(count - 1))

        @pl.when(sweep == ITERS - 1)
        def _():
            relays(sides[-1:], rear)
            send_share()

        consume(sweep, parity, 0)
        pl.when(sweep < ITERS - 1)(lambda: relays(sides[-1:], rear))
        for piece in range(1, count):
            consume(sweep, parity, piece)
        for mask in stages[1] + sides:
            drain(0, mask)

    @pl.loop(0, ITERS + 1)
    def _(sweep):
        parity = lax.rem(sweep, 2)
        solve(sweep, parity)
        pl.when(sweep < ITERS)(lambda: exchange(sweep, parity))

    save = pltpu.make_async_copy(final, out.at[0], load_sem.at[0])
    save.start()
    for bits in range(1, bodies):
        share(bits).wait_recv()
    total = jnp.zeros((8, 128), F32)
    for body in range(bodies):
        total = total + shares[differ(me, body, bodies)]
    force[0] = total[0:2, 0:heads]
    for bits in range(1, bodies):
        share(bits).wait_send()
    save.wait()


def solution(mesh):
    bodies = mesh.shape["body"]

    def step(incident, self_inverse, cross_blocks, neighbours, panel_weight):
        heads, panels = incident.shape[2:]
        slots = neighbours.shape[1]
        rows = 2 * heads
        count = panels // TILE
        vmem = pl.BlockSpec(memory_space=pltpu.VMEM)
        anywhere = pl.BlockSpec(memory_space=pl.ANY)
        return pl.pallas_call(
            functools.partial(kernel, bodies, slots, heads, panels),
            out_shape=(
                jax.ShapeDtypeStruct(incident.shape, F32),
                jax.ShapeDtypeStruct((1, 2, heads), F32),
            ),
            in_specs=[pl.BlockSpec(memory_space=pltpu.SMEM), vmem, anywhere, anywhere, vmem],
            out_specs=(anywhere, vmem),
            scratch_shapes=[
                pltpu.VMEM((2 + 2 * slots, panels, panels), F32),
                pltpu.VMEM((2 * panels, panels), BF16),
                pltpu.VMEM((2 * panels, panels), BF16),
                pltpu.VMEM((2 * slots * panels, panels), BF16),
                pltpu.VMEM((2 * slots * panels, panels), BF16),
                pltpu.VMEM((2 * rows, 2 * slots * TILE), BF16),
                pltpu.VMEM((2 * rows, 2 * panels), BF16),
                pltpu.VMEM((rows, panels), F32),
                pltpu.VMEM((2, heads, panels), F32),
                pltpu.VMEM((bodies, 8, 128), F32),
                pltpu.VMEM((16, panels), BF16),
                pltpu.VMEM((8, panels), F32),
                pltpu.VMEM((1 + slots, 8, panels), F32),
                pltpu.VMEM((rows, panels), F32),
                pltpu.SemaphoreType.DMA((2 + 2 * slots,)),
                pltpu.SemaphoreType.DMA((bodies.bit_length(), bodies, count)),
                pltpu.SemaphoreType.DMA((2, bodies, count)),
                pltpu.SemaphoreType.DMA((bodies,)),
                pltpu.SemaphoreType.DMA((bodies,)),
                *[pltpu.VMEM((bodies, rows, TILE), F32)] * (2 * count),
            ],
            compiler_params=pltpu.CompilerParams(
                collective_id=0, has_side_effects=True, vmem_limit_bytes=60 * 1024 * 1024
            ),
        )(neighbours, incident, self_inverse, cross_blocks, panel_weight)

    return jax.shard_map(
        step,
        mesh=mesh,
        in_specs=(
            P(("farm", "body"), None, None, None),
            P(("farm", "body"), None, None, None),
            P(("farm", "body"), None, None, None, None),
            P(("farm", "body"), None),
            P(("farm", "body"), None),
        ),
        out_specs=(P(("farm", "body"), None, None, None), P("farm", None, None)),
        check_vma=False,
    )
```

```python
import functools

import jax
import jax.numpy as jnp
from jax import lax
from jax.experimental import pallas as pl
from jax.experimental.pallas import tpu as pltpu
from jax.sharding import PartitionSpec as P

ITERS = 6
TILE = 256
VIA = (2,)
F32 = jnp.float32
BF16 = jnp.bfloat16


def flip(index, bits):
    bit = 1
    while bit <= bits:
        if bits & bit:
            index = index + bit - 2 * bit * ((index // bit) % 2)
        bit *= 2
    return index


def differ(first, second, bodies):
    total, bit = 0, 1
    while bit < bodies:
        total = total + bit * (((first // bit) + (second // bit)) % 2)
        bit *= 2
    return total


def halves(value):
    high = value.astype(BF16)
    return high, (value - high.astype(F32)).astype(BF16)


def put_field(lhs, column, value, heads):
    rows, width = value.shape
    high, low = halves(value)
    high_t = jnp.concatenate([-high[heads:], high[:heads]], axis=0)
    low_t = jnp.concatenate([-low[heads:], low[:heads]], axis=0)
    lhs[0:rows, column : column + width] = high
    lhs[rows : 2 * rows, column : column + width] = low
    lhs[0:rows, column + width : column + 2 * width] = high_t
    lhs[rows : 2 * rows, column + width : column + 2 * width] = low_t


def multiply(lhs, base, depth, high, low, at, rows):
    deep = slice(base, base + depth)
    both = jnp.dot(lhs[:, 0:depth], high[deep, at], preferred_element_type=F32)
    small = jnp.dot(lhs[0:rows, 0:depth], low[deep, at], preferred_element_type=F32)
    return both[:rows] + both[rows:] + small


def routes(bodies):
    far = [bit for bit in (2**k for k in range(20)) if 4 <= bit < bodies][::-1]
    masks = sorted(
        {sum(bit for j, bit in enumerate(far) if pick >> j & 1) for pick in range(1, 2 ** len(far))},
        key=lambda mask: (bin(mask).count("1"), -mask),
    )
    return far, masks


def kernel(
    bodies, slots, heads, panels,
    neighbours, incident, inverse, blocks, weight,
    out, force,
    stage, inv_high, inv_low, cross_high, cross_low, lhs, lhs_own, product, final, shares,
    scale, sums, pull, tally,
    load_sem, send_sem, recv_sem, share_send, share_recv, *gathered,
):
    rows = 2 * heads
    me = lax.axis_index("body")
    count = panels // TILE
    cuts = [slice(start, start + TILE) for start in range(0, panels, TILE)]
    far, masks = routes(bodies)
    last_side = masks[-1] + 2

    def load(index):
        source = inverse.at[0, index] if index < 2 else blocks.at[0, (index - 2) // 2, (index - 2) % 2]
        return pltpu.make_async_copy(source, stage.at[index], load_sem.at[index])

    for index in range(2):
        load(index).start()

    barrier = pltpu.get_barrier_semaphore()
    for bits in range(1, bodies):
        pl.semaphore_signal(barrier, inc=1, device_id={"body": flip(me, bits)})

    for index in range(2, 2 + 2 * slots):
        load(index).start()

    def split(index, high, low, part, parts):
        load(index).wait()

        @pl.loop(0, panels // 128)
        def _(step):
            at = pl.ds(pl.multiple_of(step * 128, 128), 128)
            upper, lower = halves(stage[index, at, :].T)
            for piece, cut in enumerate(cuts):
                to = parts * cut.start + part * TILE
                high[to : to + TILE, at] = upper[cut]
                low[to : to + TILE, at] = lower[cut]

    def copy(parity, mask, bit, piece):
        return pltpu.make_async_remote_copy(
            src_ref=gathered[parity * count + piece].at[mask],
            dst_ref=gathered[parity * count + piece].at[mask ^ bit],
            send_sem=send_sem.at[bit.bit_length() - 1, mask, piece],
            recv_sem=recv_sem.at[parity, mask ^ bit, piece],
            device_id={"body": flip(me, bit)},
        )

    def wait_in(parity, mask, piece):
        copy(parity, mask ^ 1, 1, piece).wait_recv()

    def onward(mask, piece):
        if mask & 1:
            return []
        if mask & 2:
            return [far[-1], 1] if mask == last_side ^ far[-1] and piece in VIA else [1]
        if mask == last_side ^ 2 and piece in VIA:
            return [1]
        low = mask & -mask if mask else 2**20
        return [bit for bit in far if bit < low] + [2, 1]

    def start(parity, mask, piece):
        for bit in onward(mask, piece):
            copy(parity, mask, bit, piece).start()

    def relay(parity, mask, piece):
        wait_in(parity, mask, piece)
        start(parity, mask, piece)

    def drain(parity, mask):
        for piece in range(count):
            for bit in onward(mask, piece):
                copy(parity, mask, bit, piece).wait_send()

    def turn(parity, act):
        for each in range(2):
            pl.when(parity == each)(functools.partial(act, each))

    def solve(sweep, parity):
        value = product[...]
        for piece, cut in enumerate(cuts):
            put_field(lhs_own, 2 * cut.start, value[:, cut], heads)
        for piece, cut in enumerate(cuts):
            part = multiply(lhs_own, 0, 2 * panels, inv_high, inv_low, cut, rows)
            final[:, :, cut] = part.reshape(2, heads, TILE)

            @pl.when(sweep < ITERS)
            def _():
                def send(each):
                    gathered[each * count + piece][0] = part
                    start(each, 0, piece)

                turn(parity, send)

    names = [neighbours[0, slot] for slot in range(slots)]
    places = [differ(jnp.maximum(name, 0), me, bodies) for name in names]

    def set_scale(value):
        scale[0:8], scale[8:16] = halves(value)

    def weigh(index):
        sums[...] = jnp.zeros_like(sums)

        @pl.loop(0, count)
        def _(step):
            at = pl.ds(pl.multiple_of(step * TILE, TILE), TILE)
            upper, lower = halves(stage[index, at, :])
            both = jnp.dot(scale[:, at], upper, preferred_element_type=F32)
            small = jnp.dot(scale[0:8, at], lower, preferred_element_type=F32)
            sums[...] += both[0:8] + both[8:16] + small

        return sums[...]

    top = lax.broadcasted_iota(jnp.int32, (8, panels), 0) == 0

    def pulled(slot, value, cut):
        turned = jnp.concatenate([-value[heads:], value[:heads]], axis=0)
        return pull[slot, 0:1, cut] * value + pull[slot, 1:2, cut] * turned

    def pull_own():
        set_scale(jnp.broadcast_to(weight[...], (8, panels)))
        real = weigh(0)
        pull[0] = jnp.where(top, real, weigh(1))
        set_scale(pull[0])
        tally[...] = pulled(0, incident[0].reshape(rows, panels), slice(0, panels))

    def pull_slot(slot):
        real, imag = weigh(2 + 2 * slot), weigh(3 + 2 * slot)
        pull[1 + slot] = jnp.where(top, real[0:1] - imag[1:2], imag[0:1] + real[1:2])

    def share(bits):
        return pltpu.make_async_remote_copy(
            src_ref=shares.at[0],
            dst_ref=shares.at[bits],
            send_sem=share_send.at[bits],
            recv_sem=share_recv.at[bits],
            device_id={"body": flip(me, bits)},
        )

    def arrive(parity, piece):
        for mask in range(1, bodies, 2):
            wait_in(parity, mask, piece)

    def held(parity, piece, slot):
        value = gathered[parity * count + piece][places[slot]]
        return jnp.where(names[slot] >= 0, value, 0.0)

    LAST = (ITERS - 1) % 2

    def send_share():
        for piece, cut in enumerate(cuts):
            arrive(LAST, piece)
            value = tally[:, cut]
            for slot in range(slots):
                value = value - pulled(1 + slot, held(LAST, piece, slot), cut)
            tally[:, cut] = value
        ones = jnp.ones((8, panels), F32)
        real, imag = [
            lax.dot_general(
                ones, tally[c * heads : (c + 1) * heads], (((1,), (1,)), ((), ())),
                precision=lax.Precision.HIGHEST, preferred_element_type=F32,
            )
            for c in range(2)
        ]
        row = lax.broadcasted_iota(jnp.int32, (8, heads), 0)
        shares[0] = jnp.zeros((8, 128), F32)
        shares[0, :, 0:heads] = jnp.where(row == 0, real, imag)
        for bits in range(1, bodies):
            share(bits).start()

    def consume(sweep, parity, piece):
        def take(each):
            if each == LAST:
                pl.when(sweep < ITERS - 1)(lambda: arrive(each, piece))
            else:
                arrive(each, piece)
            for slot in range(slots):
                put_field(lhs, 2 * slot * TILE, held(each, piece, slot), heads)

        turn(parity, take)
        depth = 2 * slots * TILE
        for cut in cuts:
            part = multiply(lhs, 2 * slots * cuts[piece].start, depth, cross_high, cross_low, cut, rows)
            before = incident[0, :, :, cut].reshape(rows, TILE) if piece == 0 else product[:, cut]
            product[:, cut] = before - part

    for part in range(2):
        split(part, inv_high, inv_low, part, 2)
    pl.semaphore_wait(barrier, bodies - 1)
    product[...] = incident[0].reshape(rows, panels)

    stages = [masks[: len(far)], masks[len(far) :]]
    sides = [mask + 2 for mask in masks]
    sides = [mask for mask in sides if mask == last_side ^ far[-1]] + [2] + [mask for mask in sides if mask != last_side ^ far[-1]]

    def exchange(sweep, parity):
        def first(parts):
            @pl.when(sweep == 0)
            def _():
                for part in parts:
                    split(2 + part, cross_high, cross_low, part, 2 * slots)

        def relays(some, which=range(count)):
            def act(each):
                for piece in which:
                    for mask in some:
                        wait_in(each, mask, piece)
                        for bit in onward(mask, piece):
                            if bit > 1:
                                copy(each, mask, bit, piece).start()
                    for mask in some:
                        copy(each, mask, 1, piece).start()

            turn(parity, act)

        total = 2 * slots
        first(range(0, (4 * total) // 8))
        for slot in range(slots):
            pl.when(sweep == 1 + slot % (ITERS - 2))(functools.partial(pull_slot, slot))
        relays(stages[0])
        first(range((4 * total) // 8, (6 * total) // 8))
        relays(stages[1])
        first(range((6 * total) // 8, total))
        pl.when(sweep == 0)(pull_own)
        relays(sides[:-1])
        for mask in [0] + stages[0]:
            drain(0, mask)
        rear = range(count - 1, count)
        relays(sides[-1:], range(count - 1))

        @pl.when(sweep == ITERS - 1)
        def _():
            relays(sides[-1:], rear)
            send_share()

        consume(sweep, parity, 0)
        pl.when(sweep < ITERS - 1)(lambda: relays(sides[-1:], rear))
        for piece in range(1, count):
            consume(sweep, parity, piece)
        for mask in stages[1] + sides:
            drain(0, mask)

    @pl.loop(0, ITERS + 1)
    def _(sweep):
        parity = lax.rem(sweep, 2)
        solve(sweep, parity)
        pl.when(sweep < ITERS)(lambda: exchange(sweep, parity))

    save = pltpu.make_async_copy(final, out.at[0], load_sem.at[0])
    save.start()
    for bits in range(1, bodies):
        share(bits).wait_recv()
    total = jnp.zeros((8, 128), F32)
    for body in range(bodies):
        total = total + shares[differ(me, body, bodies)]
    force[0] = total[0:2, 0:heads]
    for bits in range(1, bodies):
        share(bits).wait_send()
    save.wait()


def solution(mesh):
    bodies = mesh.shape["body"]

    def step(incident, self_inverse, cross_blocks, neighbours, panel_weight):
        heads, panels = incident.shape[2:]
        slots = neighbours.shape[1]
        rows = 2 * heads
        count = panels // TILE
        vmem = pl.BlockSpec(memory_space=pltpu.VMEM)
        anywhere = pl.BlockSpec(memory_space=pl.ANY)
        return pl.pallas_call(
            functools.partial(kernel, bodies, slots, heads, panels),
            out_shape=(
                jax.ShapeDtypeStruct(incident.shape, F32),
                jax.ShapeDtypeStruct((1, 2, heads), F32),
            ),
            in_specs=[pl.BlockSpec(memory_space=pltpu.SMEM), vmem, anywhere, anywhere, vmem],
            out_specs=(anywhere, vmem),
            scratch_shapes=[
                pltpu.VMEM((2 + 2 * slots, panels, panels), F32),
                pltpu.VMEM((2 * panels, panels), BF16),
                pltpu.VMEM((2 * panels, panels), BF16),
                pltpu.VMEM((2 * slots * panels, panels), BF16),
                pltpu.VMEM((2 * slots * panels, panels), BF16),
                pltpu.VMEM((2 * rows, 2 * slots * TILE), BF16),
                pltpu.VMEM((2 * rows, 2 * panels), BF16),
                pltpu.VMEM((rows, panels), F32),
                pltpu.VMEM((2, heads, panels), F32),
                pltpu.VMEM((bodies, 8, 128), F32),
                pltpu.VMEM((16, panels), BF16),
                pltpu.VMEM((8, panels), F32),
                pltpu.VMEM((1 + slots, 8, panels), F32),
                pltpu.VMEM((rows, panels), F32),
                pltpu.SemaphoreType.DMA((2 + 2 * slots,)),
                pltpu.SemaphoreType.DMA((bodies.bit_length(), bodies, count)),
                pltpu.SemaphoreType.DMA((2, bodies, count)),
                pltpu.SemaphoreType.DMA((bodies,)),
                pltpu.SemaphoreType.DMA((bodies,)),
                *[pltpu.VMEM((bodies, rows, TILE), F32)] * (2 * count),
            ],
            compiler_params=pltpu.CompilerParams(
                collective_id=0, has_side_effects=True, vmem_limit_bytes=60 * 1024 * 1024
            ),
        )(neighbours, incident, self_inverse, cross_blocks, panel_weight)

    return jax.shard_map(
        step,
        mesh=mesh,
        in_specs=(
            P(("farm", "body"), None, None, None),
            P(("farm", "body"), None, None, None),
            P(("farm", "body"), None, None, None, None),
            P(("farm", "body"), None),
            P(("farm", "body"), None),
        ),
        out_specs=(P(("farm", "body"), None, None, None), P("farm", None, None)),
        check_vma=False,
    )
```

```python
import functools

import jax
import jax.numpy as jnp
from jax import lax
from jax.experimental import pallas as pl
from jax.experimental.pallas import tpu as pltpu
from jax.sharding import PartitionSpec as P

ITERS = 6
TILE = 256
VIA = (2,)
F32 = jnp.float32
BF16 = jnp.bfloat16


def flip(index, bits):
    bit = 1
    while bit <= bits:
        if bits & bit:
            index = index + bit - 2 * bit * ((index // bit) % 2)
        bit *= 2
    return index


def differ(first, second, bodies):
    total, bit = 0, 1
    while bit < bodies:
        total = total + bit * (((first // bit) + (second // bit)) % 2)
        bit *= 2
    return total


def halves(value):
    high = value.astype(BF16)
    return high, (value - high.astype(F32)).astype(BF16)


def put_field(lhs, column, value, heads):
    rows, width = value.shape
    high, low = halves(value)
    high_t = jnp.concatenate([-high[heads:], high[:heads]], axis=0)
    low_t = jnp.concatenate([-low[heads:], low[:heads]], axis=0)
    lhs[0:rows, column : column + width] = high
    lhs[rows : 2 * rows, column : column + width] = low
    lhs[0:rows, column + width : column + 2 * width] = high_t
    lhs[rows : 2 * rows, column + width : column + 2 * width] = low_t


def multiply(lhs, base, depth, high, low, at, rows):
    deep = slice(base, base + depth)
    both = jnp.dot(lhs[:, 0:depth], high[deep, at], preferred_element_type=F32)
    small = jnp.dot(lhs[0:rows, 0:depth], low[deep, at], preferred_element_type=F32)
    return both[:rows] + both[rows:] + small


def routes(bodies):
    far = [bit for bit in (2**k for k in range(20)) if 4 <= bit < bodies][::-1]
    masks = sorted(
        {sum(bit for j, bit in enumerate(far) if pick >> j & 1) for pick in range(1, 2 ** len(far))},
        key=lambda mask: (bin(mask).count("1"), -mask),
    )
    return far, masks


def kernel(
    bodies, slots, heads, panels,
    neighbours, incident, inverse, blocks, weight,
    out, force,
    stage, inv_high, inv_low, cross_high, cross_low, lhs, lhs_own, product, final, shares,
    scale, sums, pull, tally,
    load_sem, send_sem, recv_sem, share_send, share_recv, *gathered,
):
    rows = 2 * heads
    me = lax.axis_index("body")
    count = panels // TILE
    cuts = [slice(start, start + TILE) for start in range(0, panels, TILE)]
    far, masks = routes(bodies)
    last_side = masks[-1] + 2

    def load(index):
        source = inverse.at[0, index] if index < 2 else blocks.at[0, (index - 2) // 2, (index - 2) % 2]
        return pltpu.make_async_copy(source, stage.at[index], load_sem.at[index])

    for index in range(2):
        load(index).start()

    barrier = pltpu.get_barrier_semaphore()
    for bits in range(1, bodies):
        pl.semaphore_signal(barrier, inc=1, device_id={"body": flip(me, bits)})

    def split(index, high, low, part, parts):
        load(index).wait()
        if index == 1:
            for later in range(2, 2 + 2 * slots):
                load(later).start()

        @pl.loop(0, panels // 128)
        def _(step):
            at = pl.ds(pl.multiple_of(step * 128, 128), 128)
            upper, lower = halves(stage[index, at, :].T)
            for piece, cut in enumerate(cuts):
                to = parts * cut.start + part * TILE
                high[to : to + TILE, at] = upper[cut]
                low[to : to + TILE, at] = lower[cut]

    def copy(parity, mask, bit, piece):
        return pltpu.make_async_remote_copy(
            src_ref=gathered[parity * count + piece].at[mask],
            dst_ref=gathered[parity * count + piece].at[mask ^ bit],
            send_sem=send_sem.at[bit.bit_length() - 1, mask, piece],
            recv_sem=recv_sem.at[parity, mask ^ bit, piece],
            device_id={"body": flip(me, bit)},
        )

    def wait_in(parity, mask, piece):
        copy(parity, mask ^ 1, 1, piece).wait_recv()

    def onward(mask, piece):
        if mask & 1:
            return []
        if mask & 2:
            return [far[-1], 1] if mask == last_side ^ far[-1] and piece in VIA else [1]
        if mask == last_side ^ 2 and piece in VIA:
            return [1]
        low = mask & -mask if mask else 2**20
        return [bit for bit in far if bit < low] + [2, 1]

    def start(parity, mask, piece):
        for bit in onward(mask, piece):
            copy(parity, mask, bit, piece).start()

    def relay(parity, mask, piece):
        wait_in(parity, mask, piece)
        start(parity, mask, piece)

    def drain(parity, mask):
        for piece in range(count):
            for bit in onward(mask, piece):
                copy(parity, mask, bit, piece).wait_send()

    def turn(parity, act):
        for each in range(2):
            pl.when(parity == each)(functools.partial(act, each))

    def solve(sweep, parity):
        value = product[...]
        for piece, cut in enumerate(cuts):
            put_field(lhs_own, 2 * cut.start, value[:, cut], heads)
        for piece, cut in enumerate(cuts):
            part = multiply(lhs_own, 0, 2 * panels, inv_high, inv_low, cut, rows)
            final[:, :, cut] = part.reshape(2, heads, TILE)

            @pl.when(sweep < ITERS)
            def _():
                def send(each):
                    gathered[each * count + piece][0] = part
                    start(each, 0, piece)

                turn(parity, send)

    names = [neighbours[0, slot] for slot in range(slots)]
    places = [differ(jnp.maximum(name, 0), me, bodies) for name in names]

    def set_scale(value):
        scale[0:8], scale[8:16] = halves(value)

    def weigh(index):
        sums[...] = jnp.zeros_like(sums)

        @pl.loop(0, count)
        def _(step):
            at = pl.ds(pl.multiple_of(step * TILE, TILE), TILE)
            upper, lower = halves(stage[index, at, :])
            both = jnp.dot(scale[:, at], upper, preferred_element_type=F32)
            small = jnp.dot(scale[0:8, at], lower, preferred_element_type=F32)
            sums[...] += both[0:8] + both[8:16] + small

        return sums[...]

    top = lax.broadcasted_iota(jnp.int32, (8, panels), 0) == 0

    def pulled(slot, value, cut):
        turned = jnp.concatenate([-value[heads:], value[:heads]], axis=0)
        return pull[slot, 0:1, cut] * value + pull[slot, 1:2, cut] * turned

    def pull_own():
        set_scale(jnp.broadcast_to(weight[...], (8, panels)))
        real = weigh(0)
        pull[0] = jnp.where(top, real, weigh(1))
        set_scale(pull[0])
        tally[...] = pulled(0, incident[0].reshape(rows, panels), slice(0, panels))

    def pull_slot(slot):
        real, imag = weigh(2 + 2 * slot), weigh(3 + 2 * slot)
        pull[1 + slot] = jnp.where(top, real[0:1] - imag[1:2], imag[0:1] + real[1:2])

    def share(bits):
        return pltpu.make_async_remote_copy(
            src_ref=shares.at[0],
            dst_ref=shares.at[bits],
            send_sem=share_send.at[bits],
            recv_sem=share_recv.at[bits],
            device_id={"body": flip(me, bits)},
        )

    def arrive(parity, piece):
        for mask in range(1, bodies, 2):
            wait_in(parity, mask, piece)

    def held(parity, piece, slot):
        value = gathered[parity * count + piece][places[slot]]
        return jnp.where(names[slot] >= 0, value, 0.0)

    LAST = (ITERS - 1) % 2

    def send_share():
        for piece, cut in enumerate(cuts):
            arrive(LAST, piece)
            value = tally[:, cut]
            for slot in range(slots):
                value = value - pulled(1 + slot, held(LAST, piece, slot), cut)
            tally[:, cut] = value
        ones = jnp.ones((8, panels), F32)
        real, imag = [
            lax.dot_general(
                ones, tally[c * heads : (c + 1) * heads], (((1,), (1,)), ((), ())),
                precision=lax.Precision.HIGHEST, preferred_element_type=F32,
            )
            for c in range(2)
        ]
        row = lax.broadcasted_iota(jnp.int32, (8, heads), 0)
        shares[0] = jnp.zeros((8, 128), F32)
        shares[0, :, 0:heads] = jnp.where(row == 0, real, imag)
        for bits in range(1, bodies):
            share(bits).start()

    def consume(sweep, parity, piece):
        def take(each):
            if each == LAST:
                pl.when(sweep < ITERS - 1)(lambda: arrive(each, piece))
            else:
                arrive(each, piece)
            for slot in range(slots):
                put_field(lhs, 2 * slot * TILE, held(each, piece, slot), heads)

        turn(parity, take)
        depth = 2 * slots * TILE
        for cut in cuts:
            part = multiply(lhs, 2 * slots * cuts[piece].start, depth, cross_high, cross_low, cut, rows)
            before = incident[0, :, :, cut].reshape(rows, TILE) if piece == 0 else product[:, cut]
            product[:, cut] = before - part

    for part in range(2):
        split(part, inv_high, inv_low, part, 2)
    pl.semaphore_wait(barrier, bodies - 1)
    product[...] = incident[0].reshape(rows, panels)

    stages = [masks[: len(far)], masks[len(far) :]]
    sides = [mask + 2 for mask in masks]
    sides = [mask for mask in sides if mask == last_side ^ far[-1]] + [2] + [mask for mask in sides if mask != last_side ^ far[-1]]

    def exchange(sweep, parity):
        def first(parts):
            @pl.when(sweep == 0)
            def _():
                for part in parts:
                    split(2 + part, cross_high, cross_low, part, 2 * slots)

        def relays(some, which=range(count)):
            def act(each):
                for piece in which:
                    for mask in some:
                        wait_in(each, mask, piece)
                        for bit in onward(mask, piece):
                            if bit > 1:
                                copy(each, mask, bit, piece).start()
                    for mask in some:
                        copy(each, mask, 1, piece).start()

            turn(parity, act)

        total = 2 * slots
        first(range(0, (4 * total) // 8))
        for slot in range(slots):
            pl.when(sweep == 1 + slot % (ITERS - 2))(functools.partial(pull_slot, slot))
        relays(stages[0])
        first(range((4 * total) // 8, (6 * total) // 8))
        relays(stages[1])
        first(range((6 * total) // 8, total))
        pl.when(sweep == 0)(pull_own)
        relays(sides[:-1])
        for mask in [0] + stages[0]:
            drain(0, mask)
        rear = range(count - 1, count)
        relays(sides[-1:], range(count - 1))

        @pl.when(sweep == ITERS - 1)
        def _():
            relays(sides[-1:], rear)
            send_share()

        consume(sweep, parity, 0)
        pl.when(sweep < ITERS - 1)(lambda: relays(sides[-1:], rear))
        for piece in range(1, count):
            consume(sweep, parity, piece)
        for mask in stages[1] + sides:
            drain(0, mask)

    @pl.loop(0, ITERS + 1)
    def _(sweep):
        parity = lax.rem(sweep, 2)
        solve(sweep, parity)
        pl.when(sweep < ITERS)(lambda: exchange(sweep, parity))

    save = pltpu.make_async_copy(final, out.at[0], load_sem.at[0])
    save.start()
    for bits in range(1, bodies):
        share(bits).wait_recv()
    total = jnp.zeros((8, 128), F32)
    for body in range(bodies):
        total = total + shares[differ(me, body, bodies)]
    force[0] = total[0:2, 0:heads]
    for bits in range(1, bodies):
        share(bits).wait_send()
    save.wait()


def solution(mesh):
    bodies = mesh.shape["body"]

    def step(incident, self_inverse, cross_blocks, neighbours, panel_weight):
        heads, panels = incident.shape[2:]
        slots = neighbours.shape[1]
        rows = 2 * heads
        count = panels // TILE
        vmem = pl.BlockSpec(memory_space=pltpu.VMEM)
        anywhere = pl.BlockSpec(memory_space=pl.ANY)
        return pl.pallas_call(
            functools.partial(kernel, bodies, slots, heads, panels),
            out_shape=(
                jax.ShapeDtypeStruct(incident.shape, F32),
                jax.ShapeDtypeStruct((1, 2, heads), F32),
            ),
            in_specs=[pl.BlockSpec(memory_space=pltpu.SMEM), vmem, anywhere, anywhere, vmem],
            out_specs=(anywhere, vmem),
            scratch_shapes=[
                pltpu.VMEM((2 + 2 * slots, panels, panels), F32),
                pltpu.VMEM((2 * panels, panels), BF16),
                pltpu.VMEM((2 * panels, panels), BF16),
                pltpu.VMEM((2 * slots * panels, panels), BF16),
                pltpu.VMEM((2 * slots * panels, panels), BF16),
                pltpu.VMEM((2 * rows, 2 * slots * TILE), BF16),
                pltpu.VMEM((2 * rows, 2 * panels), BF16),
                pltpu.VMEM((rows, panels), F32),
                pltpu.VMEM((2, heads, panels), F32),
                pltpu.VMEM((bodies, 8, 128), F32),
                pltpu.VMEM((16, panels), BF16),
                pltpu.VMEM((8, panels), F32),
                pltpu.VMEM((1 + slots, 8, panels), F32),
                pltpu.VMEM((rows, panels), F32),
                pltpu.SemaphoreType.DMA((2 + 2 * slots,)),
                pltpu.SemaphoreType.DMA((bodies.bit_length(), bodies, count)),
                pltpu.SemaphoreType.DMA((2, bodies, count)),
                pltpu.SemaphoreType.DMA((bodies,)),
                pltpu.SemaphoreType.DMA((bodies,)),
                *[pltpu.VMEM((bodies, rows, TILE), F32)] * (2 * count),
            ],
            compiler_params=pltpu.CompilerParams(
                collective_id=0, has_side_effects=True, vmem_limit_bytes=60 * 1024 * 1024
            ),
        )(neighbours, incident, self_inverse, cross_blocks, panel_weight)

    return jax.shard_map(
        step,
        mesh=mesh,
        in_specs=(
            P(("farm", "body"), None, None, None),
            P(("farm", "body"), None, None, None),
            P(("farm", "body"), None, None, None, None),
            P(("farm", "body"), None),
            P(("farm", "body"), None),
        ),
        out_specs=(P(("farm", "body"), None, None, None), P("farm", None, None)),
        check_vma=False,
    )
```
